128 devices in a mesh: section: 8 (over x, core), expert: 16 (over y, z).
Axes of the slice: x: 4, y: 4, z: 4, core: 2. Of those that a mesh axis runs over, the one named last changes fastest.
Arguments:
- arriving: bfloat16 [16384, 2560], P(('section', 'expert')), may hold values from -6 to 6
- expert_id: int32 [16384, 1], P(('section', 'expert')), may hold values from 0 to 15; in each aligned block of 128 rows (0 to 127, 128 to 255, ...) at most 10 rows name the same one
- router: bfloat16 [2560, 16], replicated, may hold values from -0.125 to 0.125
- gate_weight: bfloat16 [16, 2560, 6144], P('expert', None, 'section'), may hold values from -0.125 to 0.125
- up_weight: bfloat16 [16, 2560, 6144], P('expert', None, 'section'), may hold values from -0.125 to 0.125
- down_weight: bfloat16 [16, 6144, 2560], P('expert', 'section'), may hold values from -0.078125 to 0.078125
- shared_gate: bfloat16 [2560, 6144], P(None, 'section'), may hold values from -0.125 to 0.125
- shared_up: bfloat16 [2560, 6144], P(None, 'section'), may hold values from -0.125 to 0.125
- shared_down: bfloat16 [6144, 2560], P('section'), may hold values from -0.078125 to 0.078125
Outputs:
- mixed: bfloat16 [16384, 2560], P(('section', 'expert'))
The draws below stay inside these ranges and needn't reach their ends.
Inputs may be any that keep to these rules, and one draw needn't show every extreme that they name: `expert_id`: among the 128 rows of one device no expert is named more than 10 times, and in every draw some expert is named exactly 10 times by the rows of some device; every expert is named by some row.
All inputs are finite; a program needn't handle non-finite values.
Results may differ from the reference program's by a relative error of at most 0.0049.
Values may be sent and summed in bfloat16 or wider, within the bound.
A program may use at most 192 MiB of HBM per device.

```python
import math
import jax
import jax.numpy as jnp
import numpy as np
from jax import lax

D = 2560
FF = 6144
SFF = 6144
TOK_DEV = 128
EXPERTS = 16
CAP = 10
ROWS = 16384
N_EXPERT = 16


def steps_of(stream_key, extent, cuts, least, high):
    def one(dim, blocks):
        draws = jax.random.uniform(jax.random.fold_in(jax.random.fold_in(stream_key, 6), dim), (blocks,), jnp.float32, least / len(cuts), high / len(cuts))
        return jnp.repeat(jnp.exp(draws), extent[dim] // blocks).reshape((-1,) + (1,) * (len(extent) - dim - 1))

    loudness = one(*cuts[0])
    for cut in cuts[1:]:
        loudness = loudness * one(*cut)
    return loudness


def assign_block(own_key, own, number, rows, number_of, top, reach, skew):
    ranking = jax.random.permutation(own_key, number_of)
    crowded, usual = portions_of(number_of, rows * top, reach, skew, True), portions_of(number_of, rows * top, reach, skew, False)
    places = jnp.arange(number_of)

    def named(sizes, offset_by):
        used = int((sizes > 0).sum())
        fixed = max(1, used // 4)
        moved = fixed + (places - fixed + offset_by * (used - fixed)) % max(1, number_of - fixed)
        return jnp.zeros((number_of,), jnp.int32).at[ranking[jnp.where(places < fixed, places, moved)]].set(jnp.asarray(sizes, jnp.int32))

    sizes = jnp.where(number % 4 == 0, named(crowded, number // 4), named(usual, number - number // 4 - 1))
    mixed = jax.random.permutation(jax.random.fold_in(own, 3), number_of)
    giver, receiver = mixed[0:number_of // 2 * 2:2], mixed[1:number_of // 2 * 2:2]
    slack = jnp.minimum(sizes[giver] - 1, reach - sizes[receiver]) // 2
    slack = jnp.where((giver == ranking[0]) | (receiver == ranking[0]) | (sizes[receiver] == 0), 0, jnp.maximum(slack, 0))
    moved = jax.random.randint(jax.random.fold_in(own, 4), (number_of // 2,), 0, 1 << 20) % (slack + 1)
    sizes = sizes.at[giver].add(-moved).at[receiver].add(moved)
    items = jnp.searchsorted(jnp.cumsum(sizes), jnp.arange(rows * top), side="right").astype(jnp.int32)
    listing = items.reshape(top, rows).T
    listing = listing[jax.random.permutation(jax.random.fold_in(own, 1), rows)]
    offset_by = jax.random.randint(jax.random.fold_in(own, 2), (rows, 1), 0, top)
    return jnp.take_along_axis(listing, (jnp.arange(top)[None, :] + offset_by) % top, axis=1)


def portions_of(number_of, total, bound, slope, full):
    weights = [(1 << 20) // math.isqrt(grade ** slope) + 1 for grade in range(1, number_of + 1)]
    largest = bound if full else min(bound, max(-(-total // number_of), total * weights[0] // sum(weights)))
    least = 1 if total - largest >= number_of - 1 else 0
    given, surplus = [largest] + [least] * (number_of - 1), total - largest - least * (number_of - 1)
    while surplus > 0:
        movable = [i for i in range(1, number_of) if given[i] < largest] or [i for i in range(1, number_of) if given[i] < bound]
        mass, remaining = sum([weights[i] for i in movable]), surplus
        for i in movable:
            addition = min(bound - given[i], max(1, remaining * weights[i] // mass), surplus)
            given[i] = given[i] + addition
            surplus = surplus - addition
    return np.array(given)


def normal_values(own_key, dims, spread, reach, pieces=(), held_as=jnp.bfloat16):
    level = steps_of(own_key, dims, pieces, -0.22, 0.18) if pieces else 1.0
    drawn = jax.random.normal(own_key, dims, jnp.float32) * spread * level
    return jnp.minimum(jnp.maximum(drawn, -reach), reach).astype(held_as)


def setup_inputs(seed: int = 0) -> dict:
    key_of = jax.random.split(jax.random.key(seed), 10)
    arriving = normal_values(key_of[0], (ROWS, D), 1.0, 6.0, ((0, 128),))
    expert_id_keys = jax.random.split(jax.random.fold_in(key_of[1], 1), ROWS // TOK_DEV)
    expert_id_turns = jax.random.permutation(jax.random.fold_in(key_of[1], 3), ROWS // TOK_DEV)
    expert_id = jax.vmap(lambda own, number: assign_block(jax.random.fold_in(key_of[1], 2), own, number, TOK_DEV, EXPERTS, 1, CAP, 2))(expert_id_keys, expert_id_turns).reshape((ROWS, 1))
    router = normal_values(key_of[2], (D, EXPERTS), D ** -0.5, 0.125)
    gate_weight = normal_values(key_of[3], (EXPERTS, D, FF), D ** -0.5, 0.125, ((0, 16), (2, 8)))
    up_weight = normal_values(key_of[4], (EXPERTS, D, FF), D ** -0.5, 0.125, ((0, 16), (2, 8)))
    down_weight = normal_values(key_of[5], (EXPERTS, FF, D), FF ** -0.5, 0.078125, ((0, 16), (1, 8)))
    shared_gate = normal_values(key_of[6], (D, SFF), D ** -0.5, 0.125, ((1, 8),))
    shared_up = normal_values(key_of[7], (D, SFF), D ** -0.5, 0.125, ((1, 8),))
    shared_down = normal_values(key_of[8], (SFF, D), SFF ** -0.5, 0.078125, ((0, 8),))
    return dict(arriving=arriving, expert_id=expert_id, router=router, gate_weight=gate_weight, up_weight=up_weight, down_weight=down_weight, shared_gate=shared_gate, shared_up=shared_up, shared_down=shared_down)


def swiglu(row_block, gate_mat, up_mat):
    gate_part = jnp.dot(row_block, gate_mat, preferred_element_type=jnp.float32)
    up_part = jnp.dot(row_block, up_mat, preferred_element_type=jnp.float32)
    return (jax.nn.silu(gate_part) * up_part).astype(jnp.bfloat16)


def reference(arriving, expert_id, router, gate_weight, up_weight, down_weight, shared_gate, shared_up, shared_down):
    stride = TOK_DEV * N_EXPERT
    tokens = jnp.roll(arriving, stride, axis=0)
    chosen = expert_id[:, 0].astype(jnp.int32)
    scores = jnp.dot(tokens, router, preferred_element_type=jnp.float32)
    picked = jnp.take_along_axis(scores, chosen[:, None], axis=1)[:, 0]
    gate_prob = jax.nn.sigmoid(picked)

    order = jnp.argsort(chosen, stable=True).astype(jnp.int32)
    expert_ids = jnp.arange(EXPERTS, dtype=jnp.int32)
    counts = jnp.sum((chosen[:, None] == expert_ids[None, :]).astype(jnp.int32), axis=0, dtype=jnp.int32)
    padded = ((counts + 127) // 128) * 128
    pad_start = (jnp.cumsum(padded, dtype=jnp.int32) - padded).astype(jnp.int32)
    raw_start = (jnp.cumsum(counts, dtype=jnp.int32) - counts).astype(jnp.int32)
    total_slots = ROWS + EXPERTS * 128
    position = jnp.arange(total_slots, dtype=jnp.int32)
    owner = jnp.sum((position[:, None] >= pad_start[None, :]).astype(jnp.int32), axis=1, dtype=jnp.int32) - 1
    local = position - pad_start[owner]
    valid = local < counts[owner]
    source = order[jnp.clip(raw_start[owner] + local, 0, ROWS - 1)]
    source_valid = jnp.where(valid, source, ROWS).astype(jnp.int32)
    block_owner = owner.reshape(total_slots // 128, 128)[:, 0]
    block_source = source_valid.reshape(total_slots // 128, 128)

    def one_block(packed):
        which, row_ids = packed
        row_block = jnp.take(tokens, row_ids, axis=0, mode="fill", fill_value=0)
        hidden = swiglu(row_block, gate_weight[which], up_weight[which])
        return jnp.dot(hidden, down_weight[which], preferred_element_type=jnp.float32)

    results = lax.map(one_block, (block_owner, block_source))
    routed = jnp.zeros((ROWS, D), jnp.float32).at[source_valid].set(results.reshape(total_slots, D), mode="drop")

    def shared_block(row_block):
        hidden = swiglu(row_block, shared_gate, shared_up)
        return jnp.dot(hidden, shared_down, preferred_element_type=jnp.float32)

    shared_out = lax.map(shared_block, tokens.reshape(ROWS // 512, 512, D)).reshape(ROWS, D)
    return (shared_out + gate_prob[:, None] * routed).astype(jnp.bfloat16)
```

```python
import jax
import jax.numpy as jnp
from jax import lax
from jax.experimental import pallas as pl
from jax.experimental.pallas import tpu as pltpu
from jax.sharding import PartitionSpec as P

MESH = pl.DeviceIdType.MESH
F32 = jnp.float32
BF16 = jnp.bfloat16

SECTIONS = 8
EXPERTS = 16
TOK = 128
CAP = 10
GROUP = 16
SLOTS = EXPERTS * CAP
PACKED = EXPERTS * GROUP
D = 2560
HALF = D // 2
HEAD = 896
TAIL = HALF - HEAD
HID = 768


def iota(shape, dim):
    return lax.broadcasted_iota(jnp.int32, shape, dim)


def picks(cond):
    return jnp.where(cond, 1.0, 0.0).astype(BF16)


def chosen_rows(pick, values):
    return jnp.dot(pick, values, preferred_element_type=F32)


def pack(head, low, high, rows):
    first = chosen_rows(head, rows[:, :HEAD])
    tail = rows[:, HEAD:]
    return (
        (first[:, :TAIL] + chosen_rows(low, tail)).astype(BF16),
        (first[:, TAIL : 2 * TAIL] + chosen_rows(high, tail)).astype(BF16),
        first[:, 2 * TAIL :].astype(BF16),
    )


def unpack(head, low, high, packed):
    first = chosen_rows(head, packed)
    tail = chosen_rows(low, packed[:, :TAIL]) + chosen_rows(high, packed[:, TAIL : 2 * TAIL])
    return first.astype(BF16), tail.astype(BF16)


def slot_maps(slot, place):
    group = (slot * 205) >> 11
    rank = slot - group * CAP
    base = slot + 6 * group
    return (
        picks(place == base),
        picks((place == base + 10) & (rank < 6)),
        picks((place == base + 4) & (rank >= 6)),
    )


def kernel(
    tok_hbm, id_ref, router_hbm, wg_hbm, wu_hbm, wd_hbm, sg_hbm, su_hbm, sd_hbm,
    out_ref,
    tok, router, wg, wu, wd, sg, su, sd,
    pos_out, pos_in, going, coming, back_going, back_coming,
    x, hid, z, y_out, y_in, r_out, r_in,
    load_sem, pos_send, pos_recv, go_send, go_recv, back_send, back_recv,
    t_send, t_recv, pair_send, pair_recv, y_send, y_recv, r_send, r_recv,
):
    s = lax.axis_index("section")
    h = lax.axis_index("expert")
    core = lax.rem(s, 2)
    sibling = s + 1 - 2 * core
    ahead = lax.rem(s + 2 * (1 - 2 * core) + SECTIONS, SECTIONS)
    behind = lax.rem(s - 2 * (1 - 2 * core) + SECTIONS, SECTIONS)
    following = lax.rem(s + 1, SECTIONS)
    previous = lax.rem(s + SECTIONS - 1, SECTIONS)

    barrier = pltpu.get_barrier_semaphore()

    def greet(j, carry):
        pl.semaphore_signal(barrier, 1, device_id={"expert": lax.rem(h + j, EXPERTS)}, device_id_type=MESH)
        return carry

    for partner in (ahead, behind, following, previous):
        pl.semaphore_signal(barrier, 1, device_id={"section": partner}, device_id_type=MESH)
    lax.fori_loop(1, EXPERTS, greet, 0)

    loads = [
        pltpu.make_async_copy(source, target, load_sem.at[number])
        for number, (source, target) in enumerate(
            [(tok_hbm, tok), (router_hbm, router), (sg_hbm, sg), (su_hbm, su), (wg_hbm, wg), (wu_hbm, wu), (sd_hbm, sd), (wd_hbm, wd)]
        )
    ]
    for load in loads:
        load.start()

    chosen = id_ref[...]
    onehot = chosen == iota((TOK, TOK), 1)
    earlier = picks(iota((TOK, TOK), 1) < iota((TOK, TOK), 0))
    before = jnp.dot(earlier, picks(onehot), preferred_element_type=F32)
    rank = jnp.sum(jnp.where(onehot, before, 0.0), axis=1, keepdims=True)
    place = chosen.astype(F32) * GROUP + rank
    pos_out[...] = jnp.broadcast_to(place, (TOK, TOK)).T[:8]

    pl.semaphore_wait(barrier, EXPERTS - 1 + 4)

    def remote(source, target, send, recv, **where):
        return pltpu.make_async_remote_copy(
            src_ref=source, dst_ref=target, send_sem=send, recv_sem=recv, device_id=where, device_id_type=MESH
        )

    pos_copy = remote(pos_out, pos_in, pos_send, pos_recv, section=previous)
    pos_copy.start()
    loads[0].wait()
    pos_copy.wait_recv()

    def group(ref, q, e):
        return ref.at[q, pl.ds(pl.multiple_of(e * GROUP, GROUP), GROUP)]

    def exchange(source, target, send, recv, q):
        def one(j, carry):
            e = lax.rem(h + j, EXPERTS)
            remote(group(source, q, e), group(target, q, h), send.at[q, e], recv.at[q, h], expert=e).start()
            return carry

        lax.fori_loop(1, EXPERTS, one, 0)
        pltpu.make_async_copy(group(source, q, h), group(target, q, h), recv.at[q, h]).start()

    def exchanged(source, target, send, recv, q):
        def one(j, carry):
            e = lax.rem(h + j, EXPERTS)
            remote(group(source, q, e), group(target, q, e), send.at[q, e], recv.at[q, e], expert=e).wait_recv()
            return carry

        lax.fori_loop(1, EXPERTS, one, 0)
        pltpu.make_async_copy(group(source, q, h), group(target, q, h), recv.at[q, h]).wait()

    def exchange_sent(source, target, send, recv, q):
        def one(j, carry):
            e = lax.rem(h + j, EXPERTS)
            remote(group(source, q, e), group(target, q, e), send.at[q, e], recv.at[q, e], expert=e).wait_send()
            return carry

        lax.fori_loop(1, EXPERTS, one, 0)

    goes = (going, coming, go_send, go_recv)
    returns = (back_going, back_coming, back_send, back_recv)

    where = pos_in[0:1, :].astype(jnp.int32)
    spot = iota((PACKED, TOK), 0)
    in_tail = (spot & (GROUP - 1)) >= CAP
    to_packed = (picks(spot == where), picks((spot == where + 10) & in_tail), picks((spot == where + 4) & in_tail))

    def put(target, q, pieces):
        target[q, :, :TAIL] = pieces[0]
        target[q, :, TAIL : 2 * TAIL] = pieces[1]
        target[q, :, 2 * TAIL :] = pieces[2]

    for q in range(2):
        put(going, q, pack(*to_packed, tok[:, q * HALF : (q + 1) * HALF]))
        exchange(*goes, q)

    own_rows, pair_rows = pl.ds(0, SLOTS), pl.ds(SLOTS, SLOTS)

    def columns(q):
        return pl.ds(q * HALF, HALF)

    def gather_step(step, q):
        source, target, device = ((0, 1, ahead), (1, 2, ahead), (0, 3, behind))[step]
        return remote(
            x.at[source, own_rows, columns(q)], x.at[target, own_rows, columns(q)],
            t_send.at[step, q], t_recv.at[step, q], section=device,
        )

    def to_pair(stage, q):
        return remote(
            x.at[stage, own_rows, columns(q)], x.at[stage, pair_rows, columns(q)],
            pair_send.at[stage, q], pair_recv.at[stage, q], section=sibling,
        )

    from_packed = slot_maps(iota((SLOTS, PACKED), 0), iota((SLOTS, PACKED), 1))
    for q in range(2):
        exchanged(*goes, q)
        first, tail = unpack(*from_packed, coming[q])
        x[0, 0:SLOTS, q * HALF : q * HALF + HEAD] = first
        x[0, 0:SLOTS, q * HALF + HEAD : (q + 1) * HALF] = tail
        gather_step(0, q).start()
        to_pair(0, q).start()
    for load in loads[1:]:
        load.wait()

    def hidden(stage):
        scores = jnp.dot(x[stage], router[...], preferred_element_type=F32)
        score = jnp.sum(jnp.where(iota(scores.shape, 1) == h, scores, 0.0), axis=1, keepdims=True)
        prob = 1.0 / (1.0 + jnp.exp(-score))
        for gate_mat, up_mat, first, scale in ((sg, su, 0, None), (wg, wu, HID, prob)):
            gate = jnp.dot(x[stage], gate_mat[...], preferred_element_type=F32)
            up = jnp.dot(x[stage], up_mat[...], preferred_element_type=F32)
            value = gate / (1.0 + jnp.exp(-gate)) * up
            if scale is not None:
                value = value * scale
            hid[:, first : first + HID] = value.astype(BF16)

    def partial_copy(stage, q):
        return remote(
            y_out.at[stage, :, columns(q)], y_in.at[stage, :, columns(q)],
            y_send.at[stage, q], y_recv.at[stage, q], section=sibling,
        )

    def down(stage):
        for q in range(2):
            cols = slice(q * HALF, (q + 1) * HALF)
            total = jnp.dot(hid[:, :HID], sd[:, cols], preferred_element_type=F32)
            total += jnp.dot(hid[:, HID:], wd[:, cols], preferred_element_type=F32)
            y_out[stage, :, cols] = total[:SLOTS].astype(BF16)
            partial_copy(stage, q).start()
            z[stage, :, cols] = total[SLOTS:]

    def settle(stage, q):
        partial_copy(stage, q).wait_recv()
        cols = slice(q * HALF, (q + 1) * HALF)
        z[stage, :, cols] += y_in[stage, :, cols].astype(F32)

    def reduce_step(step, q):
        device = (behind, ahead, ahead)[step]
        return remote(
            r_out.at[step, :, columns(q)], r_in.at[step, :, columns(q)],
            r_send.at[step, q], r_recv.at[step, q], section=device,
        )

    def send_sum(step, stage, q):
        cols = slice(q * HALF, (q + 1) * HALF)
        r_out[step, :, cols] = z[stage, :, cols].astype(BF16)
        reduce_step(step, q).start()

    def send_joined(q):
        reduce_step(1, q).wait_recv()
        cols = slice(q * HALF, (q + 1) * HALF)
        r_out[2, :, cols] = (z[core, :, cols] + r_in[1, :, cols].astype(F32)).astype(BF16)
        reduce_step(2, q).start()

    def pass_on(step, stage, forward):
        for q in range(2):
            gather_step(step, q).wait_recv()
            if forward is not None:
                gather_step(forward, q).start()
            to_pair(stage, q).start()

    def ready(stage):
        for q in range(2):
            to_pair(stage, q).wait_recv()

    ready(0)
    hidden(0)
    down(0)

    pass_on(0, 1, 1)
    for q in range(2):
        settle(0, q)
    ready(1)
    hidden(1)
    for q in range(2):
        gather_step(2, q).start()
    down(1)

    pass_on(1, 2, None)
    for q in range(2):
        settle(1, q)

    @pl.when(core == 0)
    def _():
        for q in range(2):
            send_sum(1, 1, q)

    ready(2)
    hidden(2)
    down(2)

    pass_on(2, 3, None)
    for q in range(2):
        settle(2, q)

    @pl.when(core == 1)
    def _():
        for q in range(2):
            send_sum(1, 2, q)

    ready(3)
    hidden(3)

    @pl.when(core == 0)
    def _():
        for q in range(2):
            send_joined(q)
        for q in range(2):
            send_sum(0, 2, q)

    down(3)
    for q in range(2):
        settle(3, q)

    @pl.when(core == 1)
    def _():
        for q in range(2):
            send_sum(0, 3, q)
        for q in range(2):
            send_joined(q)

    last = lax.rem(3 + core, 4)
    back_packed = slot_maps(iota((PACKED, SLOTS), 1), iota((PACKED, SLOTS), 0))
    for q in range(2):
        reduce_step(0, q).wait_recv()
        reduce_step(2, q).wait_recv()
        cols = slice(q * HALF, (q + 1) * HALF)
        final = z[last, :, cols] + r_in[0, :, cols].astype(F32) + r_in[2, :, cols].astype(F32)
        put(back_going, q, pack(*back_packed, final.astype(BF16)))
        exchange(*returns, q)

    chosen_place = place.astype(jnp.int32)
    spot = iota((TOK, PACKED), 1)
    low_rank = rank < 6.0
    home = (
        picks(spot == chosen_place),
        picks((spot == chosen_place + 10) & low_rank),
        picks((spot == chosen_place + 4) & jnp.logical_not(low_rank)),
    )
    for q in range(2):
        exchanged(*returns, q)
        first, tail = unpack(*home, back_coming[q])
        out_ref[:, q * HALF : q * HALF + HEAD] = first
        out_ref[:, q * HALF + HEAD : (q + 1) * HALF] = tail

    pos_copy.wait_send()
    for q in range(2):
        exchange_sent(*goes, q)
        exchange_sent(*returns, q)
        for step in range(3):
            gather_step(step, q).wait_send()
            reduce_step(step, q).wait_send()
        for stage in range(4):
            to_pair(stage, q).wait_send()
            partial_copy(stage, q).wait_send()


def on_device(arriving, expert_id, router, gate_weight, up_weight, down_weight, shared_gate, shared_up, shared_down):
    anywhere = pl.BlockSpec(memory_space=pl.ANY)
    vmem = pl.BlockSpec(memory_space=pltpu.VMEM)
    dma = pltpu.SemaphoreType.DMA
    rows = 8 * SLOTS
    return pl.pallas_call(
        kernel,
        out_shape=jax.ShapeDtypeStruct((TOK, D), BF16),
        in_specs=[anywhere, vmem] + [anywhere] * 7,
        out_specs=vmem,
        scratch_shapes=[
            pltpu.VMEM((TOK, D), BF16),
            pltpu.VMEM((D, EXPERTS), BF16),
            pltpu.VMEM((D, HID), BF16),
            pltpu.VMEM((D, HID), BF16),
            pltpu.VMEM((HID, D), BF16),
            pltpu.VMEM((D, HID), BF16),
            pltpu.VMEM((D, HID), BF16),
            pltpu.VMEM((HID, D), BF16),
            pltpu.VMEM((8, TOK), F32),
            pltpu.VMEM((8, TOK), F32),
            pltpu.VMEM((2, PACKED, HEAD), BF16),
            pltpu.VMEM((2, PACKED, HEAD), BF16),
            pltpu.VMEM((2, PACKED, HEAD), BF16),
            pltpu.VMEM((2, PACKED, HEAD), BF16),
            pltpu.VMEM((4, 2 * SLOTS, D), BF16),
            pltpu.VMEM((2 * SLOTS, 2 * HID), BF16),
            pltpu.VMEM((4, SLOTS, D), F32),
            pltpu.VMEM((4, SLOTS, D), BF16),
            pltpu.VMEM((4, SLOTS, D), BF16),
            pltpu.VMEM((3, SLOTS, D), BF16),
            pltpu.VMEM((3, SLOTS, D), BF16),
            dma((8,)),
            dma,
            dma,
            dma((2, EXPERTS)),
            dma((2, EXPERTS)),
            dma((2, EXPERTS)),
            dma((2, EXPERTS)),
            dma((3, 2)),
            dma((3, 2)),
            dma((4, 2)),
            dma((4, 2)),
            dma((4, 2)),
            dma((4, 2)),
            dma((3, 2)),
            dma((3, 2)),
        ],
        compiler_params=pltpu.CompilerParams(
            collective_id=0, has_side_effects=True, vmem_limit_bytes=62 * 2**20
        ),
        cost_estimate=pl.CostEstimate(
            flops=2 * rows * D * HID * 6, bytes_accessed=12 * D * HID + 4 * TOK * D, transcendentals=2 * rows * HID
        ),
    )(
        arriving, expert_id, router, gate_weight[0], up_weight[0], down_weight[0], shared_gate, shared_up, shared_down
    )


def solution(mesh):
    placed = (
        P(("section", "expert"), None),
        P(("section", "expert"), None),
        P(),
        P("expert", None, "section"),
        P("expert", None, "section"),
        P("expert", "section", None),
        P(None, "section"),
        P(None, "section"),
        P("section", None),
    )
    return jax.shard_map(
        on_device,
        mesh=mesh,
        in_specs=placed,
        out_specs=P(("section", "expert"), None),
        check_vma=False,
    )
```

```python
import jax
import jax.numpy as jnp
from jax import lax
from jax.experimental import pallas as pl
from jax.experimental.pallas import tpu as pltpu
from jax.sharding import PartitionSpec as P

MESH = pl.DeviceIdType.MESH
F32 = jnp.float32
BF16 = jnp.bfloat16

SECTIONS = 8
EXPERTS = 16
TOK = 128
CAP = 10
GROUP = 16
SLOTS = EXPERTS * CAP
PACKED = EXPERTS * GROUP
D = 2560
PARTS = 5
WIDE = D // PARTS
HEAD = 384
TAIL = WIDE - HEAD
HID = 768


def iota(shape, dim):
    return lax.broadcasted_iota(jnp.int32, shape, dim)


def picks(cond):
    return jnp.where(cond, 1.0, 0.0).astype(BF16)


def chosen_rows(pick, values):
    return jnp.dot(pick, values, preferred_element_type=F32)


def pack(head, low, high, rows):
    first = chosen_rows(head, rows[:, :HEAD])
    tail = rows[:, HEAD:]
    return (
        (first[:, :TAIL] + chosen_rows(low, tail)).astype(BF16),
        (first[:, TAIL : 2 * TAIL] + chosen_rows(high, tail)).astype(BF16),
        first[:, 2 * TAIL :].astype(BF16),
    )


def unpack(head, low, high, packed):
    first = chosen_rows(head, packed)
    tail = chosen_rows(low, packed[:, :TAIL]) + chosen_rows(high, packed[:, TAIL : 2 * TAIL])
    return first.astype(BF16), tail.astype(BF16)


def slot_maps(slot, place):
    group = (slot * 205) >> 11
    rank = slot - group * CAP
    base = slot + 6 * group
    return (
        picks(place == base),
        picks((place == base + 10) & (rank < 6)),
        picks((place == base + 4) & (rank >= 6)),
    )


def kernel(
    tok_hbm, id_ref, router_hbm, wg_hbm, wu_hbm, wd_hbm, sg_hbm, su_hbm, sd_hbm,
    out_ref,
    tok, router, wg, wu, sg, su, both_down,
    pos_out, pos_in, going, coming, back_coming,
    x, hid, z, y_out, y_in, r_out, r_in,
    load_sem, pos_send, pos_recv, go_send, go_recv, back_send, back_recv,
    t_send, t_recv, pair_send, pair_recv, y_send, y_recv, r_send, r_recv,
):
    s = lax.axis_index("section")
    h = lax.axis_index("expert")
    core = lax.rem(s, 2)
    sibling = s + 1 - 2 * core
    ahead = lax.rem(s + 2 * (1 - 2 * core) + SECTIONS, SECTIONS)
    behind = lax.rem(s - 2 * (1 - 2 * core) + SECTIONS, SECTIONS)
    following = lax.rem(s + 1, SECTIONS)
    previous = lax.rem(s + SECTIONS - 1, SECTIONS)

    barrier = pltpu.get_barrier_semaphore()

    def greet(j, carry):
        pl.semaphore_signal(barrier, 1, device_id={"expert": lax.rem(h + j, EXPERTS)}, device_id_type=MESH)
        return carry

    for partner in (ahead, behind, following, previous):
        pl.semaphore_signal(barrier, 1, device_id={"section": partner}, device_id_type=MESH)
    lax.fori_loop(1, EXPERTS, greet, 0)

    loads = [
        pltpu.make_async_copy(source, target, load_sem.at[number])
        for number, (source, target) in enumerate(
            [(tok_hbm, tok), (router_hbm, router), (sg_hbm, sg), (su_hbm, su), (wg_hbm, wg), (wu_hbm, wu), (sd_hbm, both_down.at[pl.ds(0, HID)]), (wd_hbm, both_down.at[pl.ds(HID, HID)])]
        )
    ]
    for load in loads:
        load.start()

    chosen = id_ref[...]
    onehot = iota((EXPERTS, TOK), 0) == chosen
    earlier = picks(iota((TOK, TOK), 0) < iota((TOK, TOK), 1))
    before = jnp.dot(picks(onehot), earlier, preferred_element_type=F32)
    rank = jnp.sum(jnp.where(onehot, before, 0.0), axis=0, keepdims=True)
    place = chosen.astype(F32) * GROUP + rank
    pos_out[...] = jnp.broadcast_to(place, (8, TOK))

    pl.semaphore_wait(barrier, EXPERTS - 1 + 4)

    def remote(source, target, send, recv, **where):
        return pltpu.make_async_remote_copy(
            src_ref=source, dst_ref=target, send_sem=send, recv_sem=recv, device_id=where, device_id_type=MESH
        )

    pos_copy = remote(pos_out, pos_in, pos_send, pos_recv, section=previous)
    pos_copy.start()
    loads[0].wait()
    pos_copy.wait_recv()

    def group(ref, q, e):
        return ref.at[q, pl.ds(pl.multiple_of(e * GROUP, GROUP), GROUP)]

    def exchange(source, target, send, recv, q):
        def one(j, carry):
            e = lax.rem(h + j, EXPERTS)
            remote(group(source, q, e), group(target, q, h), send.at[q, e], recv.at[q, h], expert=e).start()
            return carry

        lax.fori_loop(1, EXPERTS, one, 0)
        pltpu.make_async_copy(group(source, q, h), group(target, q, h), recv.at[q, h]).start()

    def exchanged(source, target, send, recv, q):
        def one(j, carry):
            e = lax.rem(h + j, EXPERTS)
            remote(group(source, q, e), group(target, q, e), send.at[q, e], recv.at[q, e], expert=e).wait_recv()
            return carry

        lax.fori_loop(1, EXPERTS, one, 0)
        pltpu.make_async_copy(group(source, q, h), group(target, q, h), recv.at[q, h]).wait()

    def exchange_sent(source, target, send, recv, q):
        def one(j, carry):
            e = lax.rem(h + j, EXPERTS)
            remote(group(source, q, e), group(target, q, e), send.at[q, e], recv.at[q, e], expert=e).wait_send()
            return carry

        lax.fori_loop(1, EXPERTS, one, 0)

    goes = (going, coming, go_send, go_recv)
    returns = (going, back_coming, back_send, back_recv)

    where = pos_in[0:1, :].astype(jnp.int32)
    spot = iota((PACKED, TOK), 0)
    in_tail = (spot & (GROUP - 1)) >= CAP
    to_packed = (picks(spot == where), picks((spot == where + 10) & in_tail), picks((spot == where + 4) & in_tail))

    def put(target, q, pieces):
        target[q, :, :TAIL] = pieces[0]
        target[q, :, TAIL : 2 * TAIL] = pieces[1]
        target[q, :, 2 * TAIL :] = pieces[2]

    for q in range(PARTS):
        put(going, q, pack(*to_packed, tok[:, q * WIDE : (q + 1) * WIDE]))
        exchange(*goes, q)

    own_rows, pair_rows = pl.ds(0, SLOTS), pl.ds(SLOTS, SLOTS)

    def columns(q):
        return pl.ds(q * WIDE, WIDE)

    def gather_step(step, q):
        source, target, device = ((0, 1, ahead), (1, 2, ahead), (0, 3, behind))[step]
        return remote(
            x.at[source, own_rows, columns(q)], x.at[target, own_rows, columns(q)],
            t_send.at[step, q], t_recv.at[step, q], section=device,
        )

    def to_pair(stage, q):
        return remote(
            x.at[stage, own_rows, columns(q)], x.at[stage, pair_rows, columns(q)],
            pair_send.at[stage, q], pair_recv.at[stage, q], section=sibling,
        )

    def pass_on(step, q):
        gather_step(step, q).wait_recv()
        to_pair(step + 1, q).start()

    def ready(stage):
        for q in range(PARTS):
            to_pair(stage, q).wait_recv()

    def activate(first, gate, up, scale):
        value = gate / (1.0 + jnp.exp(-gate)) * up
        if scale is not None:
            value = value * scale
        hid[:, first : first + HID] = value.astype(BF16)

    def probs(stage):
        scores = lax.dot_general(x[stage], router[...], (((1,), (1,)), ((), ())), preferred_element_type=F32)
        score = jnp.sum(jnp.where(iota(scores.shape, 1) == h, scores, 0.0), axis=1, keepdims=True)
        return 1.0 / (1.0 + jnp.exp(-score))

    mats = (sg, su, wg, wu)

    def kept(number, part):
        place_of = 2 * number + part
        first = place_of % 3 * HID
        return 1 + place_of // 3, slice(first, first + HID)

    def added(number, q):
        cols = slice(q * WIDE, (q + 1) * WIDE)
        total = jnp.dot(x[0, :, cols], mats[number][cols, :], preferred_element_type=F32)
        if q == 0:
            return total
        halves = [z[kept(number, part)[0], :, kept(number, part)[1]] for part in range(2)]
        return total + jnp.concatenate(halves, axis=0)

    def widen(q):
        to_pair(0, q).wait_recv()
        for number in range(4):
            total = added(number, q)
            for part in range(2):
                level, cols = kept(number, part)
                z[level, :, cols] = total[part * SLOTS : (part + 1) * SLOTS]

    def partial_copy(stage, q):
        return remote(
            y_out.at[stage, :, columns(q)], y_in.at[stage, :, columns(q)],
            y_send.at[stage, q], y_recv.at[stage, q], section=sibling,
        )

    def down(stage, after):
        for q in range(PARTS):
            cols = slice(q * WIDE, (q + 1) * WIDE)
            total = jnp.dot(hid[...], both_down[:, cols], preferred_element_type=F32)
            y_out[stage, :, cols] = total[:SLOTS].astype(BF16)
            partial_copy(stage, q).start()
            z[stage, :, cols] = total[SLOTS:]
            after(q)

    def chip_sum(stage, q):
        partial_copy(stage, q).wait_recv()
        cols = slice(q * WIDE, (q + 1) * WIDE)
        return z[stage, :, cols] + y_in[stage, :, cols].astype(F32)

    def reduce_step(step, q):
        return remote(
            r_out.at[step, :, columns(q)], r_in.at[step, :, columns(q)],
            r_send.at[step, q], r_recv.at[step, q], section=(ahead, behind, behind)[step],
        )

    def send_sum(step, stage, q):
        r_out[step, :, q * WIDE : (q + 1) * WIDE] = chip_sum(stage, q).astype(BF16)
        reduce_step(step, q).start()

    def send_joined(stage, q):
        reduce_step(1, q).wait_recv()
        cols = slice(q * WIDE, (q + 1) * WIDE)
        r_out[2, :, cols] = (chip_sum(stage, q) + r_in[1, :, cols].astype(F32)).astype(BF16)
        reduce_step(2, q).start()

    def nothing(*_):
        pass

    def on_core(which, action, *steps):
        @pl.when(core == which)
        def _():
            for step in steps:
                action(*step)

    def hidden(stage, between):
        ready(stage)
        gate = jnp.dot(x[stage], sg[...], preferred_element_type=F32)
        up = jnp.dot(x[stage], su[...], preferred_element_type=F32)
        activate(0, gate, up, None)
        between()
        gate = jnp.dot(x[stage], wg[...], preferred_element_type=F32)
        up = jnp.dot(x[stage], wu[...], preferred_element_type=F32)
        activate(HID, gate, up, probs(stage))

    from_packed = slot_maps(iota((SLOTS, PACKED), 0), iota((SLOTS, PACKED), 1))
    for q in range(PARTS):
        exchanged(*goes, q)
        first, tail = unpack(*from_packed, coming[q])
        x[0, 0:SLOTS, q * WIDE : q * WIDE + HEAD] = first
        x[0, 0:SLOTS, q * WIDE + HEAD : (q + 1) * WIDE] = tail
        gather_step(0, q).start()
        to_pair(0, q).start()
        if q == 0:
            for load in loads[1:]:
                load.wait()
        if q >= 1:
            widen(q - 1)
        if q >= 2:
            pass_on(0, q - 2)
        if q >= 3:
            gather_step(1, q - 3).start()

    every = range(PARTS)
    last_part = PARTS - 1
    to_pair(0, last_part).wait_recv()
    activate(0, added(0, last_part), added(1, last_part), None)
    pass_on(0, last_part - 1)
    gather_step(1, last_part - 2).start()
    activate(HID, added(2, last_part), added(3, last_part), probs(0))
    pass_on(0, last_part)
    gather_step(1, last_part - 1).start()
    gather_step(1, last_part).start()
    down(0, nothing)

    for q in every:
        gather_step(2, q).start()
    hidden(1, nothing)
    for q in every:
        pass_on(1, q)
    down(1, lambda q: on_core(0, send_sum, (1, 1, q - 2)) if q >= 2 else None)

    on_core(0, send_sum, *[(0, 0, q) for q in every])
    hidden(2, lambda: on_core(0, send_sum, (1, 1, PARTS - 2), (1, 1, PARTS - 1)))
    for q in every:
        pass_on(2, q)
    down(2, lambda q: on_core(1, send_sum, (1, 2, q - 2)) if q >= 2 else None)

    on_core(1, send_sum, *[(0, 1, q) for q in every])

    def between():
        on_core(1, send_sum, (1, 2, PARTS - 2), (1, 2, PARTS - 1))
        on_core(0, send_joined, *[(2, q) for q in every])

    hidden(3, between)
    for q in every:
        exchange_sent(*goes, q)
    down(3, lambda q: on_core(1, send_joined, (3, q - 2)) if q >= 2 else None)
    on_core(1, send_joined, (3, PARTS - 2), (3, PARTS - 1))

    last = lax.rem(3 + core, 4)
    back_packed = slot_maps(iota((PACKED, SLOTS), 1), iota((PACKED, SLOTS), 0))
    chosen_place = jnp.broadcast_to(place, (TOK, TOK)).T[:, 0:1].astype(jnp.int32)
    spot = iota((TOK, PACKED), 1)
    low_rank = (chosen_place & (GROUP - 1)) < 6
    home = (
        picks(spot == chosen_place),
        picks((spot == chosen_place + 10) & low_rank),
        picks((spot == chosen_place + 4) & jnp.logical_not(low_rank)),
    )
    for q in range(PARTS):
        reduce_step(0, q).wait_recv()
        reduce_step(2, q).wait_recv()
        partial_copy(last, q).wait_recv()
        cols = slice(q * WIDE, (q + 1) * WIDE)
        final = z[last, :, cols] + y_in[last, :, cols].astype(F32)
        final += r_in[0, :, cols].astype(F32) + r_in[2, :, cols].astype(F32)
        put(going, q, pack(*back_packed, final.astype(BF16)))
        exchange(*returns, q)

    for q in range(PARTS):
        exchanged(*returns, q)
        first, tail = unpack(*home, back_coming[q])
        out_ref[:, q * WIDE : q * WIDE + HEAD] = first
        out_ref[:, q * WIDE + HEAD : (q + 1) * WIDE] = tail

    pos_copy.wait_send()
    for q in range(PARTS):
        exchange_sent(*returns, q)
        for step in range(3):
            gather_step(step, q).wait_send()
            reduce_step(step, q).wait_send()
        for stage in range(4):
            to_pair(stage, q).wait_send()
            partial_copy(stage, q).wait_send()


def on_device(arriving, expert_id, router, gate_weight, up_weight, down_weight, shared_gate, shared_up, shared_down):
    anywhere = pl.BlockSpec(memory_space=pl.ANY)
    vmem = pl.BlockSpec(memory_space=pltpu.VMEM)
    dma = pltpu.SemaphoreType.DMA
    rows = 8 * SLOTS
    return pl.pallas_call(
        kernel,
        out_shape=jax.ShapeDtypeStruct((TOK, D), BF16),
        in_specs=[anywhere, vmem] + [anywhere] * 7,
        out_specs=vmem,
        scratch_shapes=[
            pltpu.VMEM((TOK, D), BF16),
            pltpu.VMEM((EXPERTS, D), BF16),
            pltpu.VMEM((D, HID), BF16),
            pltpu.VMEM((D, HID), BF16),
            pltpu.VMEM((D, HID), BF16),
            pltpu.VMEM((D, HID), BF16),
            pltpu.VMEM((2 * HID, D), BF16),
            pltpu.VMEM((8, TOK), F32),
            pltpu.VMEM((8, TOK), F32),
            pltpu.VMEM((PARTS, PACKED, HEAD), BF16),
            pltpu.VMEM((PARTS, PACKED, HEAD), BF16),
            pltpu.VMEM((PARTS, PACKED, HEAD), BF16),
            pltpu.VMEM((4, 2 * SLOTS, D), BF16),
            pltpu.VMEM((2 * SLOTS, 2 * HID), BF16),
            pltpu.VMEM((4, SLOTS, D), F32),
            pltpu.VMEM((4, SLOTS, D), BF16),
            pltpu.VMEM((4, SLOTS, D), BF16),
            pltpu.VMEM((3, SLOTS, D), BF16),
            pltpu.VMEM((3, SLOTS, D), BF16),
            dma((8,)),
            dma,
            dma,
            dma((PARTS, EXPERTS)),
            dma((PARTS, EXPERTS)),
            dma((PARTS, EXPERTS)),
            dma((PARTS, EXPERTS)),
            dma((3, PARTS)),
            dma((3, PARTS)),
            dma((4, PARTS)),
            dma((4, PARTS)),
            dma((4, PARTS)),
            dma((4, PARTS)),
            dma((3, PARTS)),
            dma((3, PARTS)),
        ],
        compiler_params=pltpu.CompilerParams(
            collective_id=0, has_side_effects=True, vmem_limit_bytes=62 * 2**20
        ),
        cost_estimate=pl.CostEstimate(
            flops=2 * rows * D * HID * 6, bytes_accessed=12 * D * HID + 4 * TOK * D, transcendentals=2 * rows * HID
        ),
    )(
        arriving, expert_id.reshape(1, TOK), router.T, gate_weight[0], up_weight[0], down_weight[0], shared_gate, shared_up, shared_down
    )


def solution(mesh):
    placed = (
        P(("section", "expert"), None),
        P(("section", "expert"), None),
        P(),
        P("expert", None, "section"),
        P("expert", None, "section"),
        P("expert", "section", None),
        P(None, "section"),
        P(None, "section"),
        P("section", None),
    )
    return jax.shard_map(
        on_device,
        mesh=mesh,
        in_specs=placed,
        out_specs=P(("section", "expert"), None),
        check_vma=False,
    )
```

```python
import jax
import jax.numpy as jnp
from jax import lax
from jax.experimental import pallas as pl
from jax.experimental.pallas import tpu as pltpu
from jax.sharding import PartitionSpec as P

MESH = pl.DeviceIdType.MESH
F32 = jnp.float32
BF16 = jnp.bfloat16

SECTIONS = 8
EXPERTS = 16
TOK = 128
CAP = 10
GROUP = 16
SLOTS = EXPERTS * CAP
PACKED = EXPERTS * GROUP
D = 2560
PARTS = 5
WIDE = D // PARTS
HEAD = 384
TAIL = WIDE - HEAD
HID = 768


def iota(shape, dim):
    return lax.broadcasted_iota(jnp.int32, shape, dim)


def picks(cond):
    return jnp.where(cond, 1.0, 0.0).astype(BF16)


def chosen_rows(pick, values):
    return jnp.dot(pick, values, preferred_element_type=F32)


def pack(head, low, high, rows):
    first = chosen_rows(head, rows[:, :HEAD])
    tail = rows[:, HEAD:]
    return (
        (first[:, :TAIL] + chosen_rows(low, tail)).astype(BF16),
        (first[:, TAIL : 2 * TAIL] + chosen_rows(high, tail)).astype(BF16),
        first[:, 2 * TAIL :].astype(BF16),
    )


def unpack(head, low, high, packed):
    first = chosen_rows(head, packed)
    tail = chosen_rows(low, packed[:, :TAIL]) + chosen_rows(high, packed[:, TAIL : 2 * TAIL])
    return first.astype(BF16), tail.astype(BF16)


def slot_maps(slot, place):
    group = (slot * 205) >> 11
    rank = slot - group * CAP
    base = slot + 6 * group
    return (
        picks(place == base),
        picks((place == base + 10) & (rank < 6)),
        picks((place == base + 4) & (rank >= 6)),
    )


def kernel(
    tok_hbm, id_ref, router_hbm, wg_hbm, wu_hbm, wd_hbm, sg_hbm, su_hbm, sd_hbm,
    out_ref,
    tok, router, wg, wu, sg, su, both_down,
    pos_out, pos_in, going, coming, back_coming,
    x, probs, hid, z, y_out, y_in, r_out, r_in,
    load_sem, pos_send, pos_recv, go_send, go_recv, back_send, back_recv,
    t_send, t_recv, pair_send, pair_recv, prob_send, prob_recv, y_send, y_recv, r_send, r_recv,
):
    s = lax.axis_index("section")
    h = lax.axis_index("expert")
    core = lax.rem(s, 2)
    sibling = s + 1 - 2 * core
    ahead = lax.rem(s + 2 * (1 - 2 * core) + SECTIONS, SECTIONS)
    behind = lax.rem(s - 2 * (1 - 2 * core) + SECTIONS, SECTIONS)
    following = lax.rem(s + 1, SECTIONS)
    previous = lax.rem(s + SECTIONS - 1, SECTIONS)

    barrier = pltpu.get_barrier_semaphore()

    def greet(j, carry):
        pl.semaphore_signal(barrier, 1, device_id={"expert": lax.rem(h + j, EXPERTS)}, device_id_type=MESH)
        return carry

    for partner in (ahead, behind, following, previous):
        pl.semaphore_signal(barrier, 1, device_id={"section": partner}, device_id_type=MESH)
    lax.fori_loop(1, EXPERTS, greet, 0)

    loads = [
        pltpu.make_async_copy(source, target, load_sem.at[number])
        for number, (source, target) in enumerate(
            [(tok_hbm, tok), (router_hbm, router), (sg_hbm, sg), (su_hbm, su), (wg_hbm, wg), (wu_hbm, wu), (sd_hbm, both_down.at[pl.ds(0, HID)]), (wd_hbm, both_down.at[pl.ds(HID, HID)])]
        )
    ]
    for load in loads:
        load.start()

    chosen = id_ref[...]
    onehot = iota((EXPERTS, TOK), 0) == chosen
    earlier = picks(iota((TOK, TOK), 0) < iota((TOK, TOK), 1))
    before = jnp.dot(picks(onehot), earlier, preferred_element_type=F32)
    rank = jnp.sum(jnp.where(onehot, before, 0.0), axis=0, keepdims=True)
    place = chosen.astype(F32) * GROUP + rank
    pos_out[...] = jnp.broadcast_to(place, (8, TOK))

    pl.semaphore_wait(barrier, EXPERTS - 1 + 4)

    def remote(source, target, send, recv, **where):
        return pltpu.make_async_remote_copy(
            src_ref=source, dst_ref=target, send_sem=send, recv_sem=recv, device_id=where, device_id_type=MESH
        )

    pos_copy = remote(pos_out, pos_in, pos_send, pos_recv, section=previous)
    pos_copy.start()
    loads[0].wait()
    pos_copy.wait_recv()

    def group(ref, q, e):
        return ref.at[q, pl.ds(pl.multiple_of(e * GROUP, GROUP), GROUP)]

    def exchange(source, target, send, recv, q):
        def one(j, carry):
            e = lax.rem(h + j, EXPERTS)
            remote(group(source, q, e), group(target, q, h), send.at[q, e], recv.at[q, h], expert=e).start()
            return carry

        lax.fori_loop(1, EXPERTS, one, 0)
        pltpu.make_async_copy(group(source, q, h), group(target, q, h), recv.at[q, h]).start()

    def exchanged(source, target, send, recv, q):
        def one(j, carry):
            e = lax.rem(h + j, EXPERTS)
            remote(group(source, q, e), group(target, q, e), send.at[q, e], recv.at[q, e], expert=e).wait_recv()
            return carry

        lax.fori_loop(1, EXPERTS, one, 0)
        pltpu.make_async_copy(group(source, q, h), group(target, q, h), recv.at[q, h]).wait()

    def exchange_sent(source, target, send, recv, q):
        def one(j, carry):
            e = lax.rem(h + j, EXPERTS)
            remote(group(source, q, e), group(target, q, e), send.at[q, e], recv.at[q, e], expert=e).wait_send()
            return carry

        lax.fori_loop(1, EXPERTS, one, 0)

    goes = (going, coming, go_send, go_recv)
    returns = (going, back_coming, back_send, back_recv)

    where = pos_in[0:1, :].astype(jnp.int32)
    spot = iota((PACKED, TOK), 0)
    in_tail = (spot & (GROUP - 1)) >= CAP
    to_packed = (picks(spot == where), picks((spot == where + 10) & in_tail), picks((spot == where + 4) & in_tail))

    def put(target, q, pieces):
        target[q, :, :TAIL] = pieces[0]
        target[q, :, TAIL : 2 * TAIL] = pieces[1]
        target[q, :, 2 * TAIL :] = pieces[2]

    for q in range(PARTS):
        put(going, q, pack(*to_packed, tok[:, q * WIDE : (q + 1) * WIDE]))
        exchange(*goes, q)

    own_rows, pair_rows = pl.ds(0, SLOTS), pl.ds(SLOTS, SLOTS)

    def columns(q):
        return pl.ds(q * WIDE, WIDE)

    def span(q):
        return pl.ds(0, D) if q is None else columns(q)

    hops = ((0, 1, ahead), (1, 2, ahead), (0, 3, behind))

    def gather_step(step, q=None):
        source, target, device = hops[step]
        return remote(
            x.at[source, own_rows, span(q)], x.at[target, own_rows, span(q)],
            t_send.at[step, q or 0], t_recv.at[step, q or 0], section=device,
        )

    def to_pair(stage, q=None):
        return remote(
            x.at[stage, own_rows, span(q)], x.at[stage, pair_rows, span(q)],
            pair_send.at[stage, q or 0], pair_recv.at[stage, q or 0], section=sibling,
        )

    def gather_probs(step):
        source, target, device = hops[step]
        return remote(probs.at[source, 0], probs.at[target, 0], prob_send.at[step], prob_recv.at[step], section=device)

    def probs_to_pair(stage):
        return remote(probs.at[stage, 0], probs.at[stage, 1], prob_send.at[3 + stage], prob_recv.at[3 + stage], section=sibling)

    def pass_on(step, parts):
        for q in parts:
            gather_step(step, q).wait_recv()
        for q in parts:
            to_pair(step + 1, q).start()

    def pass_probs(step):
        gather_probs(step).wait_recv()
        if step == 0:
            gather_probs(1).start()
        probs_to_pair(step + 1).start()

    def ready(stage):
        for q in range(PARTS):
            to_pair(stage, q).wait_recv()

    def activate(first, gate, up, scales=None):
        value = gate / (1.0 + jnp.exp(-gate)) * up
        if scales is not None:
            for part, scale in enumerate(scales):
                rows = slice(part * SLOTS, (part + 1) * SLOTS)
                hid[rows, first : first + HID] = (value[rows] * scale).astype(BF16)
        else:
            hid[:, first : first + HID] = value.astype(BF16)

    def scales(stage):
        probs_to_pair(stage).wait_recv()
        return [jnp.broadcast_to(probs[stage, part, 0:1, :], (TOK, 2 * TOK)).T[:SLOTS, 0:1] for part in range(2)]

    mats = (sg, su, wg, wu)

    def kept(number, part):
        place_of = 2 * number + part
        first = place_of % 3 * HID
        return 1 + place_of // 3, slice(first, first + HID)

    def added(number, q):
        cols = slice(q * WIDE, (q + 1) * WIDE)
        total = jnp.dot(x[0, :, cols], mats[number][cols, :], preferred_element_type=F32)
        if q == 0:
            return total
        halves = [z[kept(number, part)[0], :, kept(number, part)[1]] for part in range(2)]
        return total + jnp.concatenate(halves, axis=0)

    def widen(q):
        to_pair(0, q).wait_recv()
        for number in range(4):
            total = added(number, q)
            for part in range(2):
                level, cols = kept(number, part)
                z[level, :, cols] = total[part * SLOTS : (part + 1) * SLOTS]

    def partial_copy(stage, q):
        return remote(
            y_out.at[stage, :, columns(q)], y_in.at[stage, :, columns(q)],
            y_send.at[stage, q], y_recv.at[stage, q], section=sibling,
        )

    def down(stage, after):
        for q in range(PARTS):
            cols = slice(q * WIDE, (q + 1) * WIDE)
            total = jnp.dot(hid[...], both_down[:, cols], preferred_element_type=F32)
            y_out[stage, :, cols] = total[:SLOTS].astype(BF16)
            partial_copy(stage, q).start()
            z[stage, :, cols] = total[SLOTS:]
            after(q)

    def chip_sum(stage, q):
        partial_copy(stage, q).wait_recv()
        cols = slice(q * WIDE, (q + 1) * WIDE)
        return z[stage, :, cols] + y_in[stage, :, cols].astype(F32)

    def reduce_step(step, q):
        return remote(
            r_out.at[step, :, span(q)], r_in.at[step, :, span(q)],
            r_send.at[step, q or 0], r_recv.at[step, q or 0], section=(ahead, behind, behind)[step],
        )

    def send_sum(step, stage, q):
        r_out[step, :, q * WIDE : (q + 1) * WIDE] = chip_sum(stage, q).astype(BF16)
        reduce_step(step, q).start()

    def send_joined(stage, q):
        reduce_step(1, q).wait_recv()
        cols = slice(q * WIDE, (q + 1) * WIDE)
        r_out[2, :, cols] = (chip_sum(stage, q) + r_in[1, :, cols].astype(F32)).astype(BF16)
        reduce_step(2, q).start()

    def nothing(*_):
        pass

    def on_core(which, action, *steps):
        @pl.when(core == which)
        def _():
            for step in steps:
                action(*step)

    def hidden(stage, between):
        ready(stage)
        gate = jnp.dot(x[stage], sg[...], preferred_element_type=F32)
        up = jnp.dot(x[stage], su[...], preferred_element_type=F32)
        activate(0, gate, up)
        between()
        gate = jnp.dot(x[stage], wg[...], preferred_element_type=F32)
        up = jnp.dot(x[stage], wu[...], preferred_element_type=F32)
        activate(HID, gate, up, scales(stage))

    from_packed = slot_maps(iota((SLOTS, PACKED), 0), iota((SLOTS, PACKED), 1))
    probs[0, 0] = jnp.zeros((8, 2 * TOK), F32)
    scores = jnp.zeros((EXPERTS, SLOTS), F32)
    for q in range(PARTS):
        exchanged(*goes, q)
        first, tail = unpack(*from_packed, coming[q])
        x[0, 0:SLOTS, q * WIDE : q * WIDE + HEAD] = first
        x[0, 0:SLOTS, q * WIDE + HEAD : (q + 1) * WIDE] = tail
        gather_step(0, q).start()
        to_pair(0, q).start()
        if q == 0:
            for load in loads[1:]:
                load.wait()
        if q >= 1:
            widen(q - 1)
        scores += lax.dot_general(
            router[:, q * WIDE : (q + 1) * WIDE], x[0, 0:SLOTS, q * WIDE : (q + 1) * WIDE],
            (((1,), (1,)), ((), ())), preferred_element_type=F32,
        )
        if q >= 2:
            pass_on(0, (q - 2,))
        if q >= 3:
            gather_step(1, q - 3).start()

    score = jnp.sum(jnp.where(iota(scores.shape, 0) == h, scores, 0.0), axis=0, keepdims=True)
    probs[0, 0, :, :SLOTS] = jnp.broadcast_to(1.0 / (1.0 + jnp.exp(-score)), (8, SLOTS))
    gather_probs(0).start()
    gather_probs(2).start()
    probs_to_pair(0).start()

    every = range(PARTS)
    last_part = PARTS - 1
    to_pair(0, last_part).wait_recv()
    activate(0, added(0, last_part), added(1, last_part))
    pass_on(0, (last_part - 1,))
    gather_step(1, last_part - 2).start()
    activate(HID, added(2, last_part), added(3, last_part), scales(0))
    pass_on(0, (last_part,))
    gather_step(1, last_part - 1).start()
    gather_step(1, last_part).start()
    pass_probs(0)
    down(0, nothing)

    for q in every:
        gather_step(2, q).start()
    hidden(1, nothing)
    pass_on(1, every)
    pass_probs(1)
    down(1, lambda q: on_core(0, send_sum, (1, 1, q - 2)) if q >= 2 else None)

    on_core(0, send_sum, (1, 1, PARTS - 2), (1, 1, PARTS - 1))
    hidden(2, lambda: on_core(0, send_sum, *[(0, 0, q) for q in every]))
    pass_on(2, every)
    pass_probs(2)
    down(2, lambda q: on_core(1, send_sum, (1, 2, q - 2)) if q >= 2 else None)

    on_core(1, send_sum, *[(0, 1, q) for q in every])

    def between():
        on_core(1, send_sum, (1, 2, PARTS - 2), (1, 2, PARTS - 1))
        on_core(0, send_joined, *[(2, q) for q in every])

    hidden(3, between)
    for q in every:
        exchange_sent(*goes, q)
    down(3, lambda q: on_core(1, send_joined, (3, q - 2)) if q >= 2 else None)
    on_core(1, send_joined, (3, PARTS - 2), (3, PARTS - 1))

    last = lax.rem(3 + core, 4)
    back_packed = slot_maps(iota((PACKED, SLOTS), 1), iota((PACKED, SLOTS), 0))
    chosen_place = jnp.broadcast_to(place, (TOK, TOK)).T[:, 0:1].astype(jnp.int32)
    spot = iota((TOK, PACKED), 1)
    low_rank = (chosen_place & (GROUP - 1)) < 6
    home = (
        picks(spot == chosen_place),
        picks((spot == chosen_place + 10) & low_rank),
        picks((spot == chosen_place + 4) & jnp.logical_not(low_rank)),
    )
    for q in range(PARTS):
        reduce_step(0, q).wait_recv()
        reduce_step(2, q).wait_recv()
        partial_copy(last, q).wait_recv()
        cols = slice(q * WIDE, (q + 1) * WIDE)
        final = z[last, :, cols] + y_in[last, :, cols].astype(F32)
        final += r_in[0, :, cols].astype(F32) + r_in[2, :, cols].astype(F32)
        put(going, q, pack(*back_packed, final.astype(BF16)))
        exchange(*returns, q)

    for q in range(PARTS):
        exchanged(*returns, q)
        first, tail = unpack(*home, back_coming[q])
        out_ref[:, q * WIDE : q * WIDE + HEAD] = first
        out_ref[:, q * WIDE + HEAD : (q + 1) * WIDE] = tail

    pos_copy.wait_send()
    for step in range(3):
        gather_probs(step).wait_send()
    for stage in range(4):
        probs_to_pair(stage).wait_send()
    for q in range(PARTS):
        exchange_sent(*returns, q)
        for step in range(2):
            gather_step(step, q).wait_send()
            reduce_step(step + 1, q).wait_send()
        reduce_step(0, q).wait_send()
        gather_step(2, q).wait_send()
        for stage in range(4):
            partial_copy(stage, q).wait_send()
            to_pair(stage, q).wait_send()


def on_device(arriving, expert_id, router, gate_weight, up_weight, down_weight, shared_gate, shared_up, shared_down):
    anywhere = pl.BlockSpec(memory_space=pl.ANY)
    vmem = pl.BlockSpec(memory_space=pltpu.VMEM)
    dma = pltpu.SemaphoreType.DMA
    rows = 8 * SLOTS
    return pl.pallas_call(
        kernel,
        out_shape=jax.ShapeDtypeStruct((TOK, D), BF16),
        in_specs=[anywhere, vmem] + [anywhere] * 7,
        out_specs=vmem,
        scratch_shapes=[
            pltpu.VMEM((TOK, D), BF16),
            pltpu.VMEM((EXPERTS, D), BF16),
            pltpu.VMEM((D, HID), BF16),
            pltpu.VMEM((D, HID), BF16),
            pltpu.VMEM((D, HID), BF16),
            pltpu.VMEM((D, HID), BF16),
            pltpu.VMEM((2 * HID, D), BF16),
            pltpu.VMEM((8, TOK), F32),
            pltpu.VMEM((8, TOK), F32),
            pltpu.VMEM((PARTS, PACKED, HEAD), BF16),
            pltpu.VMEM((PARTS, PACKED, HEAD), BF16),
            pltpu.VMEM((PARTS, PACKED, HEAD), BF16),
            pltpu.VMEM((4, 2 * SLOTS, D), BF16),
            pltpu.VMEM((4, 2, 8, 2 * TOK), F32),
            pltpu.VMEM((2 * SLOTS, 2 * HID), BF16),
            pltpu.VMEM((4, SLOTS, D), F32),
            pltpu.VMEM((4, SLOTS, D), BF16),
            pltpu.VMEM((4, SLOTS, D), BF16),
            pltpu.VMEM((3, SLOTS, D), BF16),
            pltpu.VMEM((3, SLOTS, D), BF16),
            dma((8,)),
            dma,
            dma,
            dma((PARTS, EXPERTS)),
            dma((PARTS, EXPERTS)),
            dma((PARTS, EXPERTS)),
            dma((PARTS, EXPERTS)),
            dma((3, PARTS)),
            dma((3, PARTS)),
            dma((4, PARTS)),
            dma((4, PARTS)),
            dma((7,)),
            dma((7,)),
            dma((4, PARTS)),
            dma((4, PARTS)),
            dma((3, PARTS)),
            dma((3, PARTS)),
        ],
        compiler_params=pltpu.CompilerParams(
            collective_id=0, has_side_effects=True, vmem_limit_bytes=62 * 2**20
        ),
        cost_estimate=pl.CostEstimate(
            flops=2 * rows * D * HID * 6, bytes_accessed=12 * D * HID + 4 * TOK * D, transcendentals=2 * rows * HID
        ),
    )(
        arriving, expert_id.reshape(1, TOK), router.T, gate_weight[0], up_weight[0], down_weight[0], shared_gate, shared_up, shared_down
    )


def solution(mesh):
    placed = (
        P(("section", "expert"), None),
        P(("section", "expert"), None),
        P(),
        P("expert", None, "section"),
        P("expert", None, "section"),
        P("expert", "section", None),
        P(None, "section"),
        P(None, "section"),
        P("section", None),
    )
    return jax.shard_map(
        on_device,
        mesh=mesh,
        in_specs=placed,
        out_specs=P(("section", "expert"), None),
        check_vma=False,
    )
```
